512 devices in a mesh: group: 8 (over z), tensor: 8 (over x, core), ctx: 8 (over y).
Axes of the slice: x: 4, y: 8, z: 8, core: 2. Of those that a mesh axis runs over, the one named last changes fastest.
Arguments:
- cache_keys: bfloat16 [32, 4096, 1024], P('group', 'ctx', 'tensor'), may hold values from -6 to 6
- cache_values: bfloat16 [32, 4096, 1024], P('group', 'ctx', 'tensor'), may hold values from -6 to 6
- sink_keys: bfloat16 [32, 4, 1024], P('group', None, 'tensor'), may hold values from -21 to 21
- sink_values: bfloat16 [32, 4, 1024], P('group', None, 'tensor'), may hold values from -6 to 6
- turn_queries: bfloat16 [32, 384, 12288], P('group', 'ctx', 'tensor'), may hold values from -160 to 160
- turn_keys: bfloat16 [32, 384, 1024], P('group', 'ctx', 'tensor'), may hold values from -4.5 to 4.5
- turn_values: bfloat16 [32, 384, 1024], P('group', 'ctx', 'tensor'), may hold values from -6 to 6
- decode_queries: bfloat16 [32, 2, 12288], P('group', None, 'tensor'), may hold values from -160 to 160
- decode_keys: bfloat16 [32, 2, 1024], P('group', None, 'tensor'), may hold values from -6 to 6
- decode_values: bfloat16 [32, 2, 1024], P('group', None, 'tensor'), may hold values from -6 to 6
- turn_lengths: int32 [32], P('group'), may hold values from 16 to 384, as said below
- history: int32 [32], P('group'), may hold values from 516 to 8191
- targets: int32 [32, 1], P('group'), may hold values from 0 to 7; in each aligned block of 4 rows (0 to 3, 4 to 7, ...) no two rows name the same one
Outputs:
- turn_out: bfloat16 [64, 384, 12288], P(('group', 'ctx'), None, 'tensor')
- decode_out: bfloat16 [64, 2, 12288], P(('group', 'ctx'), None, 'tensor')
- moved_keys: bfloat16 [64, 4096, 1024], P(('group', 'ctx'), None, 'tensor')
- moved_values: bfloat16 [64, 4096, 1024], P(('group', 'ctx'), None, 'tensor')
The draws below stay inside these ranges and needn't reach their ends.
Inputs may be any that keep to these rules, and one draw needn't show every extreme that they name: `turn_lengths`: some session has exactly 384 tokens and some exactly 16. `targets`: the 4 sessions of one home group (aligned blocks of 4 sessions) go to different groups.
All inputs are finite; a program needn't handle non-finite values.
Results may differ from the reference program's by a relative error of at most 0.0055.
Values may be sent and summed in bfloat16 or wider, within the bound.
A program may use at most 64 MiB of HBM per device.

```python
import math
import jax
import jax.numpy as jnp
import numpy as np
from jax import lax

HEADS = 96
KV_HEADS = 8
HEAD_DIM = 128
WINDOW = 4096
SINKS = 4
DECODE_STEPS = 2
TURN = 384
SESS_GRP = 4
SESSIONS = 32
SLOTS = 64
N_GROUP = 8


def shared_keys(key):
    base_keys = jnp.clip(jax.random.normal(jax.random.fold_in(key, 101), (SESSIONS, TURN, KV_HEADS * HEAD_DIM), jnp.float32), -4.0, 4.0)
    return base_keys


def draw_turn_keys(key, part):
    base_keys = shared_keys(key)
    return base_keys.astype(jnp.bfloat16)


def draw_turn_queries(key, part):
    key = jax.random.fold_in(key, 2)
    queries = jnp.clip(jax.random.normal(key, (SESSIONS, TURN, HEADS * HEAD_DIM), jnp.float32), -4.0, 4.0)
    return queries.astype(jnp.bfloat16)


def draw_decode_queries(key, part):
    key = jax.random.fold_in(key, 4)
    queries = jnp.clip(jax.random.normal(key, (SESSIONS, DECODE_STEPS, HEADS * HEAD_DIM), jnp.float32), -4.0, 4.0)
    return queries.astype(jnp.bfloat16)


def draw_turn_lengths(key, part):
    key = jax.random.fold_in(key, 3)
    first_key, second_key = jax.random.split(key)
    lengths = jax.random.randint(first_key, (SESSIONS,), 16, TURN + 1)
    order = jax.random.permutation(second_key, SESSIONS)
    lengths = lengths.at[order[0]].set(TURN).at[order[1]].set(16)
    return lengths.astype(jnp.int32)


def set_ends(result, key, smallest, high):
    place = [jax.random.randint(jax.random.fold_in(key, axis), (), 0, length) for axis, length in enumerate(result.shape)]
    longest = result.shape.index(max(result.shape))
    beside = place[:longest] + [(place[longest] + 1) % result.shape[longest]] + place[longest + 1:]
    return result.at[tuple(place)].set(smallest).at[tuple(beside)].set(high)


def level_of(own_key, shape, pieces, low, top_value):
    factor_of = 1.0
    for dim, blocks in pieces:
        steps = jax.random.uniform(jax.random.fold_in(jax.random.fold_in(own_key, 6), dim), (blocks,), jnp.float32, low / len(pieces), top_value / len(pieces))
        factor_of = factor_of * jnp.repeat(jnp.exp(steps), shape[dim] // blocks).reshape((-1,) + (1,) * (len(shape) - 1 - dim))
    return factor_of


def deal_out(rng, own, number, rows, amount, top, reach, lean):
    order = jax.random.permutation(rng, amount)
    packed, common = load_shares(amount, rows * top, reach, lean, True), load_shares(amount, rows * top, reach, lean, False)
    places = jnp.arange(amount)

    def named(tallies, turn):
        used = int((tallies > 0).sum())
        fixed = max(1, used // 4)
        passed = fixed + (places - fixed + turn * (used - fixed)) % max(1, amount - fixed)
        return jnp.zeros((amount,), jnp.int32).at[order[jnp.where(places < fixed, places, passed)]].set(jnp.asarray(tallies, jnp.int32))

    tallies = jnp.where(number % 4 == 0, named(packed, number // 4), named(common, number - number // 4 - 1))
    mixed = jax.random.permutation(jax.random.fold_in(own, 3), amount)
    donor, taker = mixed[0:amount // 2 * 2:2], mixed[1:amount // 2 * 2:2]
    slack = jnp.minimum(tallies[donor] - 1, reach - tallies[taker]) // 2
    slack = jnp.where((donor == order[0]) | (taker == order[0]) | (tallies[taker] == 0), 0, jnp.maximum(slack, 0))
    passed = jax.random.randint(jax.random.fold_in(own, 4), (amount // 2,), 0, 1 << 20) % (slack + 1)
    tallies = tallies.at[donor].add(-passed).at[taker].add(passed)
    members = jnp.searchsorted(jnp.cumsum(tallies), jnp.arange(rows * top), side="right").astype(jnp.int32)
    table = members.reshape(top, rows).T
    table = table[jax.random.permutation(jax.random.fold_in(own, 1), rows)]
    turn = jax.random.randint(jax.random.fold_in(own, 2), (rows, 1), 0, top)
    return jnp.take_along_axis(table, (jnp.arange(top)[None, :] + turn) % top, axis=1)


def load_shares(count, total, bound, lean, full):
    weights = [(1 << 20) // math.isqrt(grade ** lean) + 1 for grade in range(1, count + 1)]
    largest = bound if full else min(bound, max(-(-total // count), total * weights[0] // sum(weights)))
    least = 1 if total - largest >= count - 1 else 0
    given, rest = [largest] + [least] * (count - 1), total - largest - least * (count - 1)
    while rest > 0:
        movable = [i for i in range(1, count) if given[i] < largest] or [i for i in range(1, count) if given[i] < bound]
        pool, budget = sum([weights[i] for i in movable]), rest
        for i in movable:
            more = min(bound - given[i], max(1, budget * weights[i] // pool), rest)
            given[i] = given[i] + more
            rest = rest - more
    return np.array(given)


def scatter_about(stream_key, shape, deviation, reach, cuts=(), kind=jnp.bfloat16):
    drawn = jax.random.normal(stream_key, shape, jnp.float32) * deviation
    if len(cuts) > 0:
        drawn = level_of(stream_key, shape, cuts, -0.22, 0.18) * drawn
    return jnp.clip(drawn, min=-reach, max=reach).astype(kind)


def setup_inputs(seed: int = 0) -> dict:
    arg_keys = jax.random.split(jax.random.key(seed), 14)
    cache_keys = scatter_about(arg_keys[0], (SESSIONS, WINDOW, KV_HEADS * HEAD_DIM), 1.0, 6.0, ((0, 8), (1, 8), (2, 8)))
    cache_values = scatter_about(arg_keys[1], (SESSIONS, WINDOW, KV_HEADS * HEAD_DIM), 1.0, 6.0, ((0, 8), (1, 8), (2, 8)))
    sink_keys = scatter_about(arg_keys[2], (SESSIONS, SINKS, KV_HEADS * HEAD_DIM), 3.5, 21.0, ((0, 8), (2, 8)))
    sink_values = scatter_about(arg_keys[3], (SESSIONS, SINKS, KV_HEADS * HEAD_DIM), 1.0, 6.0, ((0, 8), (2, 8)))
    turn_queries = draw_turn_queries(jax.random.fold_in(arg_keys[13], 71), 0)
    turn_keys = draw_turn_keys(jax.random.fold_in(arg_keys[13], 71), 0)
    turn_values = scatter_about(arg_keys[6], (SESSIONS, TURN, KV_HEADS * HEAD_DIM), 1.0, 6.0, ((0, 8), (1, 8), (2, 8)))
    decode_queries = draw_decode_queries(jax.random.fold_in(arg_keys[13], 71), 0)
    decode_keys = scatter_about(arg_keys[8], (SESSIONS, DECODE_STEPS, KV_HEADS * HEAD_DIM), 1.0, 6.0, ((0, 8), (2, 8)))
    decode_values = scatter_about(arg_keys[9], (SESSIONS, DECODE_STEPS, KV_HEADS * HEAD_DIM), 1.0, 6.0, ((0, 8), (2, 8)))
    turn_lengths = draw_turn_lengths(jax.random.fold_in(arg_keys[13], 71), 0)
    history = set_ends(jax.random.randint(arg_keys[11], (SESSIONS,), SINKS + WINDOW // 8, 2 * WINDOW), jax.random.fold_in(arg_keys[11], 1), SINKS + WINDOW // 8, (2 * WINDOW) - 1).astype(jnp.int32)
    targets_keys = jax.random.split(jax.random.fold_in(arg_keys[12], 1), SESSIONS // SESS_GRP)
    targets_turns = jax.random.permutation(jax.random.fold_in(arg_keys[12], 3), SESSIONS // SESS_GRP)
    targets = jax.vmap(lambda own, number: deal_out(jax.random.fold_in(arg_keys[12], 2), own, number, SESS_GRP, N_GROUP, 1, 1, 0))(targets_keys, targets_turns).reshape((SESSIONS, 1))
    return {"cache_keys": cache_keys, "cache_values": cache_values, "sink_keys": sink_keys, "sink_values": sink_values, "turn_queries": turn_queries, "turn_keys": turn_keys, "turn_values": turn_values, "decode_queries": decode_queries, "decode_keys": decode_keys, "decode_values": decode_values, "turn_lengths": turn_lengths, "history": history, "targets": targets}


def attention(queries, key_rows, value_rows, visible):
    scores = jnp.einsum('grd,nd->grn', queries.astype(jnp.float32), key_rows.astype(jnp.float32)) * (1.0 / math.sqrt(HEAD_DIM))
    scores = jnp.where(visible[None], scores, -1e+30)
    peak = lax.optimization_barrier(jnp.max(scores, axis=-1, keepdims=True))
    weights = jnp.exp(scores - peak)
    weight_sum = lax.optimization_barrier(jnp.sum(weights, axis=-1, keepdims=True))
    rounded = lax.optimization_barrier(weights.astype(jnp.bfloat16)).astype(jnp.float32)
    weighted = jnp.einsum('grn,nd->grd', rounded, value_rows.astype(jnp.float32))
    return weighted / weight_sum

def reference(cache_keys, cache_values, sink_keys, sink_values, turn_queries, turn_keys, turn_values, decode_queries, decode_keys, decode_values, turn_lengths, history, targets):
    group_size = HEADS // KV_HEADS
    all_rows = SINKS + WINDOW + TURN + DECODE_STEPS
    column_ids = jnp.arange(all_rows, dtype=jnp.int32)
    in_window = (column_ids >= SINKS) & (column_ids < SINKS + WINDOW)
    in_turn = (column_ids >= SINKS + WINDOW) & (column_ids < SINKS + WINDOW + TURN)
    in_decode = column_ids >= SINKS + WINDOW + TURN
    is_sink = column_ids < SINKS
    window_ids = column_ids - SINKS
    turn_ids = column_ids - SINKS - WINDOW
    decode_ids = column_ids - SINKS - WINDOW - TURN
    row_ids = jnp.arange(TURN, dtype=jnp.int32)
    step_ids = jnp.arange(DECODE_STEPS, dtype=jnp.int32)

    def one_session(fields):
        window_k, window_v, sink_k, sink_v, query_t, key_t, value_t, query_d, key_d, value_d, length, prior = fields
        usable = in_window & (prior - WINDOW + window_ids >= SINKS)
        turn_mask = is_sink[None, :] | usable[None, :] & (window_ids[None, :] > row_ids[:, None]) | in_turn[None, :] & (turn_ids[None, :] <= row_ids[:, None])
        decode_mask = is_sink[None, :] | usable[None, :] & (window_ids[None, :] > length + step_ids[:, None]) | (in_turn[None, :] & (turn_ids[None, :] < length))[0:1] | in_decode[None, :] & (decode_ids[None, :] <= step_ids[:, None])
        key_rows = jnp.concatenate([sink_k, window_k, key_t, key_d], axis=0).reshape(all_rows, KV_HEADS, HEAD_DIM).transpose(1, 0, 2)
        value_rows = jnp.concatenate([sink_v, window_v, value_t, value_d], axis=0).reshape(all_rows, KV_HEADS, HEAD_DIM).transpose(1, 0, 2)
        turn_heads = query_t.reshape(TURN, KV_HEADS, group_size, HEAD_DIM).transpose(1, 2, 0, 3)
        decode_heads = query_d.reshape(DECODE_STEPS, KV_HEADS, group_size, HEAD_DIM).transpose(1, 2, 0, 3)

        def per_head(parts):
            turn_part, decode_part, head_keys, head_values = parts
            return (attention(turn_part, head_keys, head_values, turn_mask), attention(decode_part, head_keys, head_values, decode_mask))
        turn_result, decode_result = lax.map(per_head, (turn_heads, decode_heads, key_rows, value_rows))
        turn_result = turn_result.transpose(2, 0, 1, 3).reshape(TURN, HEADS * HEAD_DIM)
        turn_result = jnp.where((row_ids < length)[:, None], turn_result, 0.0).astype(jnp.bfloat16)
        decode_result = decode_result.transpose(2, 0, 1, 3).reshape(DECODE_STEPS, HEADS * HEAD_DIM).astype(jnp.bfloat16)
        return (turn_result, decode_result)
    home_turn, home_decode = lax.map(one_session, (cache_keys, cache_values, sink_keys, sink_values, turn_queries, turn_keys, turn_values, decode_queries, decode_keys, decode_values, turn_lengths, history))
    slot = targets[:, 0].astype(jnp.int32) * N_GROUP + jnp.arange(SESSIONS, dtype=jnp.int32) // SESS_GRP
    turn_out = jnp.zeros((SLOTS, TURN, HEADS * HEAD_DIM), jnp.bfloat16).at[slot].set(home_turn)
    decode_out = jnp.zeros((SLOTS, DECODE_STEPS, HEADS * HEAD_DIM), jnp.bfloat16).at[slot].set(home_decode)
    moved_keys = jnp.zeros((SLOTS, WINDOW, KV_HEADS * HEAD_DIM), jnp.bfloat16).at[slot].set(cache_keys)
    moved_values = jnp.zeros((SLOTS, WINDOW, KV_HEADS * HEAD_DIM), jnp.bfloat16).at[slot].set(cache_values)
    return (turn_out, decode_out, moved_keys, moved_values)
```

```python
import functools
import math

import jax
import jax.numpy as jnp
from jax import lax
from jax.experimental import pallas as pl
from jax.experimental.pallas import tpu as pltpu
from jax.sharding import PartitionSpec as P

HEAD_DIM = 128
SINKS = 4
NEG = -1e30
MESH = pl.DeviceIdType.MESH
PAD = 16
QUERY_STAGES = 6
AHEAD = 3


def kernel(
    ring,
    stages,
    lengths,
    history,
    targets,
    cache_k,
    cache_v,
    sink_k,
    sink_v,
    turn_q,
    turn_k,
    turn_v,
    decode_q,
    decode_k,
    decode_v,
    turn_out,
    decode_out,
    keys_out,
    values_out,
    send,
    stage,
    final,
    small_send,
    small_meta,
    small,
    meta,
    peak,
    total,
    bias,
    z_send,
    z_recv,
    y_send,
    y_recv,
    own_sem,
    small_send_sem,
    small_recv_sem,
    small_own_sem,
    out_sem,
):
    z = lax.axis_index("group")
    tensor = lax.axis_index("tensor")
    y = lax.axis_index("ctx")
    sessions, window_rows, _ = cache_k.shape
    turn_rows = turn_k.shape[1]
    heads = turn_q.shape[2] // HEAD_DIM
    steps = decode_q.shape[1]
    window = window_rows * ring
    turn = turn_rows * ring
    query_rows = turn + PAD
    head_rows = (heads + 2) * turn_rows
    query_size = head_rows // QUERY_STAGES
    chunk = window_rows // stages
    key_size = 2 * chunk
    width = ring * chunk
    scale = math.log2(math.e) / math.sqrt(HEAD_DIM)

    def around(place, step):
        return lax.rem(place + step + ring, ring)

    barrier = pltpu.get_barrier_semaphore()
    for step in range(1, ring):
        pl.semaphore_signal(
            barrier, inc=1, device_id=(around(z, step), tensor, y), device_id_type=MESH
        )
        pl.semaphore_signal(
            barrier, inc=1, device_id=(z, tensor, around(y, step)), device_id_type=MESH
        )

    def chosen(target):
        named = jnp.int32(0)
        active = jnp.int32(0)
        for s in range(sessions):
            hit = (targets[s] == target).astype(jnp.int32)
            named = jnp.maximum(named, s * hit)
            active = jnp.maximum(active, hit)
        return named, active

    def put(step, place, size, value):
        @pl.when(step == 0)
        def _():
            stage[0, pl.ds(place, size), :] = value

        @pl.when(step != 0)
        def _():
            send[step, pl.ds(place, size), :] = value

    def prepare_queries(step, carry):
        named, active = chosen(around(z, step))
        live = active.astype(jnp.float32).astype(jnp.bfloat16)
        for head in range(heads):
            columns = slice(head * HEAD_DIM, (head + 1) * HEAD_DIM)
            put(step, head * turn_rows, turn_rows, turn_q[named, :, columns] * live)
        put(step, heads * turn_rows, turn_rows, turn_k[named] * live)
        put(step, (heads + 1) * turn_rows, turn_rows, turn_v[named] * live)
        return carry

    def prepare_window(step, carry):
        named, active = chosen(around(z, step))
        live = active.astype(jnp.float32).astype(jnp.bfloat16)
        for number in range(stages):
            rows = slice(number * chunk, (number + 1) * chunk)
            place = head_rows + number * key_size
            put(step, place, chunk, cache_k[named, rows, :] * live)
            put(step, place + chunk, chunk, cache_v[named, rows, :] * live)
        return carry

    def prepare_small(step, carry):
        named, active = chosen(around(z, step))
        live = active.astype(jnp.float32).astype(jnp.bfloat16)
        small_send[step] = jnp.zeros(small_send.shape[1:], jnp.bfloat16)
        small_send[step, 0:SINKS, :] = sink_k[named] * live
        small_send[step, PAD : PAD + steps, :] = decode_k[named] * live
        small_send[step, 2 * PAD : 2 * PAD + SINKS, :] = sink_v[named] * live
        small_send[step, 3 * PAD : 3 * PAD + steps, :] = decode_v[named] * live
        for head in range(heads):
            columns = slice(head * HEAD_DIM, (head + 1) * HEAD_DIM)
            place = (4 + head) * PAD
            small_send[step, place : place + steps, :] = decode_q[named, :, columns] * live
        small_meta[step, 0:8, :] = jnp.full((8, 128), history[named] * active, jnp.int32)
        small_meta[step, 8:16, :] = jnp.full((8, 128), lengths[named] * active, jnp.int32)
        return carry

    lax.fori_loop(0, ring, prepare_queries, 0)

    @pl.when(z == y)
    def _():
        lax.fori_loop(0, ring, prepare_small, 0)

    pl.semaphore_wait(barrier, 2 * (ring - 1))

    def z_copy(number, place, size, step):
        rows = pl.ds(place, size)
        return pltpu.make_async_remote_copy(
            send.at[step, rows],
            stage.at[step, rows],
            z_send.at[number, step],
            z_recv.at[number, step],
            device_id=(around(z, step), tensor, y),
            device_id_type=MESH,
        )

    def y_copy(number, place, size, step, source, target):
        rows = pl.ds(place, size)
        return pltpu.make_async_remote_copy(
            stage.at[step, rows],
            final.at[source, rows],
            y_send.at[number, step],
            y_recv.at[number, source],
            device_id=(z, tensor, target),
            device_id_type=MESH,
        )

    def own_copy(number, place, size, step):
        rows = pl.ds(place, size)
        return pltpu.make_async_copy(
            stage.at[step, rows], final.at[y, rows], own_sem.at[number]
        )

    def query_part(number):
        return number, pl.multiple_of(number * query_size, 16), query_size

    def key_part(number):
        place = pl.multiple_of(head_rows + number * key_size, 16)
        return number + QUERY_STAGES, place, key_size

    steps_out = sorted(range(1, ring), key=lambda step: -min(step, ring - step))
    steps_in = [0] + steps_out[::-1]

    def spread(part):
        for step in steps_out:
            z_copy(*part, step).start()

    def forward(part):
        for step in steps_in:
            home = around(z, -step)
            if step:
                z_copy(*part, step).wait_recv()

            @pl.when(home != y)
            def _():
                y_copy(*part, step, y, home).start()

            @pl.when(home == y)
            def _():
                own_copy(*part, step).start()

    def arrive(part):
        own_copy(*part, 0).wait()
        for step in range(1, ring):
            source = around(y, step)
            y_copy(*part, 0, source, source).wait_recv()

    def small_copies(step):
        target = (around(z, step), tensor, y)
        return (
            pltpu.make_async_remote_copy(
                small_send.at[step],
                small,
                small_send_sem.at[0, step],
                small_recv_sem.at[0],
                device_id=target,
                device_id_type=MESH,
            ),
            pltpu.make_async_remote_copy(
                small_meta.at[step],
                meta,
                small_send_sem.at[1, step],
                small_recv_sem.at[1],
                device_id=target,
                device_id_type=MESH,
            ),
        )

    def small_own():
        return (
            pltpu.make_async_copy(small_send.at[0], small, small_own_sem.at[0]),
            pltpu.make_async_copy(small_meta.at[0], meta, small_own_sem.at[1]),
        )

    for number in range(AHEAD):
        spread(query_part(number))

    lax.fori_loop(0, ring, prepare_window, 0)

    @pl.when(z == y)
    def _():
        for step in steps_out:
            for copy in small_copies(step):
                copy.start()
        for copy in small_own():
            copy.start()

    def early(number, carry):
        spread(query_part(number + AHEAD))
        forward(query_part(number))
        return carry

    def late(number, carry):
        spread(key_part(number + AHEAD - QUERY_STAGES))
        forward(query_part(number))
        return carry

    lax.fori_loop(0, QUERY_STAGES - AHEAD, early, 0)
    lax.fori_loop(QUERY_STAGES - AHEAD, QUERY_STAGES, late, 0)

    def arrive_queries(number, carry):
        arrive(query_part(number))
        return carry

    for number in range(2):
        spread(key_part(number + AHEAD))
        forward(key_part(number))
    lax.fori_loop(0, QUERY_STAGES, arrive_queries, 0)

    @pl.when(z == y)
    def _():
        for copy in small_own():
            copy.wait()

    @pl.when(z != y)
    def _():
        for copy in small_copies(1):
            copy.wait_recv()

    def block_of(place, size):
        return final[:, pl.ds(place, size), :].reshape(ring * size, HEAD_DIM)

    def queries_of(head):
        extra = small[(4 + head) * PAD : (5 + head) * PAD, :]
        return jnp.concatenate([block_of(head * turn_rows, turn_rows), extra], axis=0)

    def scores_of(queries, keys):
        return lax.dot_general(
            queries,
            keys,
            (((1,), (1,)), ((), ())),
            preferred_element_type=jnp.float32,
        )

    def with_ones(values):
        return jnp.concatenate([values, jnp.ones_like(values)], axis=1)

    prior = meta[0:1, 0:1]
    length = meta[8:9, 0:1]

    def row_numbers(shape):
        return lax.broadcasted_iota(jnp.int32, shape, 0)

    def column_numbers(shape):
        return lax.broadcasted_iota(jnp.int32, shape, 1)

    first = (query_rows, turn + 2 * PAD)
    row, column = row_numbers(first), column_numbers(first)
    in_turn = row < turn
    limit = jnp.where(in_turn, row, length - 1)
    number = column - turn - PAD
    sees = (
        ((column < turn) & (column <= limit))
        | ((column >= turn) & (column < turn + SINKS))
        | ((number >= 0) & (number < steps) & (number <= row - turn))
    )
    bias[...] = jnp.where(sees, 0.0, NEG)
    first_keys = jnp.concatenate(
        [block_of(heads * turn_rows, turn_rows), small[0 : 2 * PAD, :]], axis=0
    )
    first_values = with_ones(
        jnp.concatenate(
            [block_of((heads + 1) * turn_rows, turn_rows), small[2 * PAD : 4 * PAD, :]], axis=0
        )
    )

    def start_head(head):
        scores = scores_of(queries_of(head), first_keys) + bias[...]
        top = jnp.max(scores, axis=1, keepdims=True)
        weights = jnp.exp2((scores - top) * scale).astype(jnp.bfloat16)
        peak[head] = jnp.broadcast_to(top, (query_rows, HEAD_DIM))
        total[head] = jnp.dot(weights, first_values, preferred_element_type=jnp.float32)

    for head in range(heads):
        start_head(head)

    def out_copies(number):
        place = pl.multiple_of(head_rows + number * key_size, 16)
        rows = pl.ds(pl.multiple_of(number * chunk, 16), chunk)
        return (
            pltpu.make_async_copy(
                final.at[:, pl.ds(place, chunk)], keys_out.at[:, rows], out_sem.at[0, number]
            ),
            pltpu.make_async_copy(
                final.at[:, pl.ds(place + chunk, chunk)],
                values_out.at[:, rows],
                out_sem.at[1, number],
            ),
        )

    def consume(number):
        arrive(key_part(number))
        for copy in out_copies(number):
            copy.start()
        place = pl.multiple_of(head_rows + number * key_size, 16)
        values = with_ones(block_of(place + chunk, chunk))
        shape = (width, HEAD_DIM)
        row, column = row_numbers(shape), column_numbers(shape)
        position = lax.div(row, chunk) * window_rows + number * chunk + lax.rem(row, chunk)
        gone = (column == 0) & (position < window + SINKS - prior)
        marked = (column == row + 1) & (row < chunk)
        marks = jnp.where(gone, NEG, jnp.where(marked, 1.0, 0.0)).astype(jnp.bfloat16)
        keys = jnp.concatenate([block_of(place, chunk), marks], axis=1)
        shape = (query_rows, HEAD_DIM)
        row, column = row_numbers(shape), column_numbers(shape)
        limit = jnp.where(row < turn, row, length + row - turn)
        passed = (column >= 1) & (number * chunk + column - 1 <= limit)
        flags = jnp.where(column == 0, 1.0, jnp.where(passed, NEG, 0.0)).astype(jnp.bfloat16)

        def one_head(head):
            scores = scores_of(jnp.concatenate([queries_of(head), flags], axis=1), keys)
            before = peak[head]
            top = jnp.maximum(before, jnp.max(scores, axis=1, keepdims=True))
            spread_top = jnp.concatenate([top] * (width // HEAD_DIM), axis=1)
            weights = jnp.exp2((scores - spread_top) * scale).astype(jnp.bfloat16)
            factor = jnp.exp2((before - top) * scale)
            peak[head] = top
            total[head] = total[head] * jnp.concatenate([factor] * 2, axis=1) + jnp.dot(
                weights, values, preferred_element_type=jnp.float32
            )

        for head in range(heads):
            one_head(head)

    def round_trip(number, carry):
        @pl.when(number + AHEAD < stages)
        def _():
            spread(key_part(number + AHEAD))

        @pl.when(number < stages)
        def _():
            forward(key_part(number))

        consume(number - 2)
        return carry

    lax.fori_loop(2, stages + 2, round_trip, 0)

    shown = row_numbers((turn, HEAD_DIM)) < length
    for head in range(heads):
        columns = slice(head * HEAD_DIM, (head + 1) * HEAD_DIM)
        result = total[head, :, 0:HEAD_DIM] / total[head, :, HEAD_DIM : 2 * HEAD_DIM]
        turn_out[:, columns] = jnp.where(shown, result[0:turn], 0.0).astype(jnp.bfloat16)
        decode_out[:, columns] = result[turn : turn + steps].astype(jnp.bfloat16)

    def finish(part):
        for step in range(ring):
            if step:
                z_copy(*part, step).wait_send()
            home = around(z, -step)

            @pl.when(home != y)
            def _():
                y_copy(*part, step, y, home).wait_send()

    def finish_queries(number, carry):
        finish(query_part(number))
        return carry

    def finish_keys(number, carry):
        finish(key_part(number))
        for copy in out_copies(number):
            copy.wait()
        return carry

    lax.fori_loop(0, QUERY_STAGES, finish_queries, 0)
    lax.fori_loop(0, stages, finish_keys, 0)

    @pl.when(z == y)
    def _():
        for step in steps_out:
            for copy in small_copies(step):
                copy.wait_send()


def shards(
    cache_keys,
    cache_values,
    sink_keys,
    sink_values,
    turn_queries,
    turn_keys,
    turn_values,
    decode_queries,
    decode_keys,
    decode_values,
    turn_lengths,
    history,
    targets,
):
    ring = lax.axis_size("ctx")
    window_rows = cache_keys.shape[1]
    turn_rows = turn_keys.shape[1]
    columns = turn_queries.shape[2]
    heads = columns // HEAD_DIM
    steps = decode_queries.shape[1]
    stages = 8
    query_rows = ring * turn_rows + PAD
    rows = (heads + 2) * turn_rows + 2 * window_rows
    small_rows = (4 + heads) * PAD
    count = QUERY_STAGES + stages
    vmem = pl.BlockSpec(memory_space=pltpu.VMEM)
    smem = pl.BlockSpec(memory_space=pltpu.SMEM)
    hbm = pl.BlockSpec(memory_space=pl.ANY)
    turn_out, decode_out, keys_out, values_out = pl.pallas_call(
        functools.partial(kernel, ring, stages),
        out_shape=(
            jax.ShapeDtypeStruct((ring * turn_rows, columns), jnp.bfloat16),
            jax.ShapeDtypeStruct((steps, columns), jnp.bfloat16),
            jax.ShapeDtypeStruct((ring, window_rows, HEAD_DIM), jnp.bfloat16),
            jax.ShapeDtypeStruct((ring, window_rows, HEAD_DIM), jnp.bfloat16),
        ),
        in_specs=[smem] * 3 + [vmem] * 10,
        out_specs=(vmem, vmem, hbm, hbm),
        scratch_shapes=[
            pltpu.VMEM((ring, rows, HEAD_DIM), jnp.bfloat16),
            pltpu.VMEM((ring, rows, HEAD_DIM), jnp.bfloat16),
            pltpu.VMEM((ring, rows, HEAD_DIM), jnp.bfloat16),
            pltpu.VMEM((ring, small_rows, HEAD_DIM), jnp.bfloat16),
            pltpu.VMEM((ring, 16, HEAD_DIM), jnp.int32),
            pltpu.VMEM((small_rows, HEAD_DIM), jnp.bfloat16),
            pltpu.VMEM((16, HEAD_DIM), jnp.int32),
            pltpu.VMEM((heads, query_rows, HEAD_DIM), jnp.float32),
            pltpu.VMEM((heads, query_rows, 2 * HEAD_DIM), jnp.float32),
            pltpu.VMEM((query_rows, ring * turn_rows + 2 * PAD), jnp.float32),
            pltpu.SemaphoreType.DMA((count, ring)),
            pltpu.SemaphoreType.DMA((count, ring)),
            pltpu.SemaphoreType.DMA((count, ring)),
            pltpu.SemaphoreType.DMA((count, ring)),
            pltpu.SemaphoreType.DMA((count,)),
            pltpu.SemaphoreType.DMA((2, ring)),
            pltpu.SemaphoreType.DMA((2,)),
            pltpu.SemaphoreType.DMA((2,)),
            pltpu.SemaphoreType.DMA((2, stages)),
        ],
        compiler_params=pltpu.CompilerParams(
            collective_id=0, has_side_effects=True, vmem_limit_bytes=56 * 1024 * 1024
        ),
    )(
        turn_lengths,
        history,
        targets[:, 0],
        cache_keys,
        cache_values,
        sink_keys,
        sink_values,
        turn_queries,
        turn_keys,
        turn_values,
        decode_queries,
        decode_keys,
        decode_values,
    )
    return (
        turn_out[None],
        decode_out[None],
        keys_out.reshape(1, ring * window_rows, HEAD_DIM),
        values_out.reshape(1, ring * window_rows, HEAD_DIM),
    )


def solution(mesh):
    whole = P("group", "ctx", "tensor")
    front = P("group", None, "tensor")
    slots = P(("group", "ctx"), None, "tensor")
    return jax.shard_map(
        shards,
        mesh=mesh,
        in_specs=(
            whole,
            whole,
            front,
            front,
            whole,
            whole,
            whole,
            front,
            front,
            front,
            P("group"),
            P("group"),
            P("group", None),
        ),
        out_specs=(slots,) * 4,
        check_vma=False,
    )
```

```python
import functools
import math

import jax
import jax.numpy as jnp
from jax import lax
from jax.experimental import pallas as pl
from jax.experimental.pallas import tpu as pltpu
from jax.sharding import PartitionSpec as P

HEAD_DIM = 128
SINKS = 4
NEG = -1e30
MESH = pl.DeviceIdType.MESH
PAD = 16
BLOCKS = 8
AHEAD = 3
BEHIND = 2


def kernel(
    ring,
    lengths,
    history,
    targets,
    cache_k_in,
    cache_v_in,
    sink_k_in,
    sink_v_in,
    turn_q_in,
    turn_k_in,
    turn_v_in,
    decode_q_in,
    decode_k_in,
    decode_v_in,
    turn_out,
    decode_out,
    keys_out,
    values_out,
    send,
    stage,
    final,
    cache_k,
    cache_v,
    sink_k,
    sink_v,
    turn_q,
    turn_k,
    turn_v,
    decode_q,
    decode_k,
    decode_v,
    in_sem,
    small_send,
    small_meta,
    small,
    meta,
    extra,
    peak,
    total,
    bias,
    z_send,
    z_recv,
    y_send,
    y_recv,
    own_sem,
    small_send_sem,
    small_recv_sem,
    small_own_sem,
    out_sem,
):
    z = lax.axis_index("group")
    tensor = lax.axis_index("tensor")
    y = lax.axis_index("ctx")
    sessions, window_rows, _ = cache_k.shape
    turn_rows = turn_k.shape[1]
    heads = turn_q.shape[2] // HEAD_DIM
    steps = decode_q.shape[1]
    window = window_rows * ring
    turn = turn_rows * ring
    query_rows = turn + PAD
    head_rows = (heads + 2) * turn_rows
    chunk = window_rows // BLOCKS
    whole = BLOCKS - 1
    query_stages = (heads + 2 - 2) // 2 + 2
    cuts = [(number * chunk, chunk) for number in range(whole)]
    cuts += [(whole * chunk + half * chunk // 2, chunk // 2) for half in range(2)]
    scale = math.log2(math.e) / math.sqrt(HEAD_DIM)

    def around(place, step):
        return lax.rem(place + step + ring, ring)

    def load(number, source, place):
        return pltpu.make_async_copy(source, place, in_sem.at[number])

    query_loads = (
        load(0, turn_q_in, turn_q),
        load(1, turn_k_in, turn_k),
        load(2, turn_v_in, turn_v),
    )
    window_loads = (load(3, cache_k_in, cache_k), load(4, cache_v_in, cache_v))
    small_loads = (
        load(5, sink_k_in, sink_k),
        load(6, sink_v_in, sink_v),
        load(7, decode_q_in, decode_q),
        load(8, decode_k_in, decode_k),
        load(9, decode_v_in, decode_v),
    )
    for copy in query_loads + small_loads + window_loads:
        copy.start()

    barrier = pltpu.get_barrier_semaphore()
    for step in range(1, ring):
        pl.semaphore_signal(
            barrier, inc=1, device_id=(around(z, step), tensor, y), device_id_type=MESH
        )
        pl.semaphore_signal(
            barrier, inc=1, device_id=(z, tensor, around(y, step)), device_id_type=MESH
        )

    def chosen(target):
        named = jnp.int32(0)
        active = jnp.int32(0)
        for s in range(sessions):
            hit = (targets[s] == target).astype(jnp.int32)
            named = jnp.maximum(named, s * hit)
            active = jnp.maximum(active, hit)
        return named, active

    def prepare_queries(step, place):
        named, active = chosen(around(z, step))
        live = active.astype(jnp.float32).astype(jnp.bfloat16)
        for head in range(heads):
            columns = slice(head * HEAD_DIM, (head + 1) * HEAD_DIM)
            rows = slice(head * turn_rows, (head + 1) * turn_rows)
            place[step, rows, :] = turn_q[named, :, columns] * live
        rows = slice(heads * turn_rows, (heads + 1) * turn_rows)
        place[step, rows, :] = turn_k[named] * live
        rows = slice((heads + 1) * turn_rows, (heads + 2) * turn_rows)
        place[step, rows, :] = turn_v[named] * live

    def prepare_window(step, place):
        named, active = chosen(around(z, step))
        live = active.astype(jnp.float32).astype(jnp.bfloat16)
        for start, size in cuts:
            rows = slice(start, start + size)
            first = head_rows + 2 * start
            place[step, first : first + size, :] = cache_k[named, rows, :] * live
            place[step, first + size : first + 2 * size, :] = cache_v[named, rows, :] * live

    def prepare(part):
        part(0, stage)

        def one_step(step, carry):
            part(step, send)
            return carry

        lax.fori_loop(1, ring, one_step, 0)

    def prepare_small(step, carry):
        named, active = chosen(around(z, step))
        live = active.astype(jnp.float32).astype(jnp.bfloat16)
        small_send[step] = jnp.zeros(small_send.shape[1:], jnp.bfloat16)
        small_send[step, 0:SINKS, :] = sink_k[named] * live
        small_send[step, PAD : PAD + steps, :] = decode_k[named] * live
        small_send[step, 2 * PAD : 2 * PAD + SINKS, :] = sink_v[named] * live
        small_send[step, 3 * PAD : 3 * PAD + steps, :] = decode_v[named] * live
        for head in range(heads):
            columns = slice(head * HEAD_DIM, (head + 1) * HEAD_DIM)
            start = 4 * PAD + head * steps
            small_send[step, start : start + steps, :] = decode_q[named, :, columns] * live
        first_row = lax.broadcasted_iota(jnp.int32, small_meta.shape[1:], 0) == 0
        small_meta[step] = jnp.where(first_row, history[named], lengths[named]) * active
        return carry

    for copy in query_loads:
        copy.wait()
    prepare(prepare_queries)

    pl.semaphore_wait(barrier, 2 * (ring - 1))

    def z_copy(number, place, size, step):
        rows = pl.ds(place, size)
        return pltpu.make_async_remote_copy(
            send.at[step, rows],
            stage.at[step, rows],
            z_send.at[number, step],
            z_recv.at[number, step],
            device_id=(around(z, step), tensor, y),
            device_id_type=MESH,
        )

    def y_copy(number, place, size, step, source, target):
        rows = pl.ds(place, size)
        return pltpu.make_async_remote_copy(
            stage.at[step, rows],
            final.at[source, rows],
            y_send.at[number, step],
            y_recv.at[number, source],
            device_id=(z, tensor, target),
            device_id_type=MESH,
        )

    def own_copy(number, place, size, step):
        rows = pl.ds(place, size)
        return pltpu.make_async_copy(
            stage.at[step, rows], final.at[y, rows], own_sem.at[number]
        )

    def short_part(number):
        return number, number * turn_rows, turn_rows

    def query_part(number):
        return number, pl.multiple_of((number - 1) * 2 * turn_rows, 16), 2 * turn_rows

    def key_part(number):
        place = pl.multiple_of(head_rows + number * 2 * chunk, 16)
        return number + query_stages, place, 2 * chunk

    def end_part(half):
        return query_stages + whole + half, head_rows + 2 * cuts[whole + half][0], chunk

    steps_out = sorted(range(1, ring), key=lambda step: -min(step, ring - step))
    steps_in = [0] + steps_out[::-1]

    def spread(part):
        for step in steps_out:
            z_copy(*part, step).start()

    def forward(part):
        for step in steps_in:
            home = around(z, -step)
            if step:
                z_copy(*part, step).wait_recv()

            @pl.when(home != y)
            def _():
                y_copy(*part, step, y, home).start()

            @pl.when(home == y)
            def _():
                own_copy(*part, step).start()

    def arrive(part):
        own_copy(*part, 0).wait()
        for step in range(1, ring):
            source = around(y, step)
            y_copy(*part, 0, source, source).wait_recv()

    def finish(part):
        for step in range(ring):
            if step:
                z_copy(*part, step).wait_send()
            home = around(z, -step)

            @pl.when(home != y)
            def _():
                y_copy(*part, step, y, home).wait_send()

    def small_copies(step):
        target = (around(z, step), tensor, y)
        return (
            pltpu.make_async_remote_copy(
                small_send.at[step],
                small,
                small_send_sem.at[0, step],
                small_recv_sem.at[0],
                device_id=target,
                device_id_type=MESH,
            ),
            pltpu.make_async_remote_copy(
                small_meta.at[step],
                meta,
                small_send_sem.at[1, step],
                small_recv_sem.at[1],
                device_id=target,
                device_id_type=MESH,
            ),
        )

    def small_own():
        return (
            pltpu.make_async_copy(small_send.at[0], small, small_own_sem.at[0]),
            pltpu.make_async_copy(small_meta.at[0], meta, small_own_sem.at[1]),
        )

    for part in (short_part(0), short_part(1), query_part(2)):
        spread(part)

    for copy in window_loads:
        copy.wait()
    prepare(prepare_window)
    for copy in small_loads:
        copy.wait()

    @pl.when(z == y)
    def _():
        lax.fori_loop(0, ring, prepare_small, 0)
        for step in steps_out:
            for copy in small_copies(step):
                copy.start()
        for copy in small_own():
            copy.start()

    def early(number, carry):
        spread(query_part(number + AHEAD))
        forward(query_part(number))
        return carry

    def late(number, carry):
        spread(key_part(number + AHEAD - query_stages))
        forward(query_part(number))
        return carry

    for number in range(2):
        spread(query_part(number + AHEAD))
        forward(short_part(number))
    lax.fori_loop(2, query_stages - AHEAD, early, 0)
    lax.fori_loop(query_stages - AHEAD, query_stages, late, 0)
    for number in range(BEHIND):
        spread(key_part(number + AHEAD))
        forward(key_part(number))

    def settle_queries(number, carry):
        arrive(query_part(number))
        finish(query_part(number))
        return carry

    for number in range(2):
        arrive(short_part(number))
        finish(short_part(number))
    lax.fori_loop(2, query_stages, settle_queries, 0)

    @pl.when(z == y)
    def _():
        for copy in small_own():
            copy.wait()

    @pl.when(z != y)
    def _():
        for copy in small_copies(1):
            copy.wait_recv()

    def block_of(place, size):
        return final[:, pl.ds(place, size), :].reshape(ring * size, HEAD_DIM)

    def queries_of(head):
        return jnp.concatenate([block_of(head * turn_rows, turn_rows), extra[head]], axis=0)

    def scores_of(queries, keys):
        return lax.dot_general(
            queries,
            keys,
            (((1,), (1,)), ((), ())),
            preferred_element_type=jnp.float32,
        )

    def with_ones(values):
        return jnp.concatenate([values, jnp.ones_like(values)], axis=1)

    prior = meta[0:1, 0:1]
    length = meta[1:2, 0:1]

    def row_numbers(shape):
        return lax.broadcasted_iota(jnp.int32, shape, 0)

    def column_numbers(shape):
        return lax.broadcasted_iota(jnp.int32, shape, 1)

    first = (query_rows, turn + 2 * PAD)
    row, column = row_numbers(first), column_numbers(first)
    in_turn = row < turn
    limit = jnp.where(in_turn, row, length - 1)
    number = column - turn - PAD
    sees = (
        ((column < turn) & (column <= limit))
        | ((column >= turn) & (column < turn + SINKS))
        | ((number >= 0) & (number < steps) & (number <= row - turn))
    )
    bias[...] = jnp.where(sees, 0.0, NEG)
    packed = small[4 * PAD :, :]
    shape = (PAD, packed.shape[0])
    row, column = row_numbers(shape), column_numbers(shape)
    for head in range(heads):
        picks = (row < steps) & (column == head * steps + row)
        picks = jnp.where(picks, 1.0, 0.0).astype(jnp.bfloat16)
        extra[head] = jnp.dot(picks, packed, preferred_element_type=jnp.float32).astype(
            jnp.bfloat16
        )
    first_keys = jnp.concatenate(
        [block_of(heads * turn_rows, turn_rows), small[0 : 2 * PAD, :]], axis=0
    )
    first_values = with_ones(
        jnp.concatenate(
            [block_of((heads + 1) * turn_rows, turn_rows), small[2 * PAD : 4 * PAD, :]], axis=0
        )
    )

    def start_head(head):
        scores = scores_of(queries_of(head), first_keys) + bias[...]
        top = jnp.max(scores, axis=1, keepdims=True)
        weights = jnp.exp2((scores - top) * scale).astype(jnp.bfloat16)
        peak[head] = jnp.broadcast_to(top, (query_rows, HEAD_DIM))
        total[head] = jnp.dot(weights, first_values, preferred_element_type=jnp.float32)

    for head in range(heads):
        start_head(head)

    shown = row_numbers((turn, HEAD_DIM)) < length

    def out_copies(start, size, number):
        place = head_rows + 2 * start
        rows = pl.ds(pl.multiple_of(start, 16), size)
        return (
            pltpu.make_async_copy(
                final.at[:, pl.ds(pl.multiple_of(place, 16), size)],
                keys_out.at[:, rows],
                out_sem.at[0, number],
            ),
            pltpu.make_async_copy(
                final.at[:, pl.ds(pl.multiple_of(place + size, 16), size)],
                values_out.at[:, rows],
                out_sem.at[1, number],
            ),
        )

    def consume(part, start, size, number, last):
        arrive(part)
        for copy in out_copies(start, size, number):
            copy.start()
        width = ring * size
        place = pl.multiple_of(head_rows + 2 * start, 16)
        values = with_ones(block_of(pl.multiple_of(place + size, 16), size))
        shape = (width, HEAD_DIM)
        row, column = row_numbers(shape), column_numbers(shape)
        position = lax.div(row, size) * window_rows + start + lax.rem(row, size)
        gone = (column == 0) & (position < window + SINKS - prior)
        marked = (column == row + 1) & (row < size)
        marks = jnp.where(gone, NEG, jnp.where(marked, 1.0, 0.0)).astype(jnp.bfloat16)
        keys = jnp.concatenate([block_of(place, size), marks], axis=1)
        shape = (query_rows, HEAD_DIM)
        row, column = row_numbers(shape), column_numbers(shape)
        limit = jnp.where(row < turn, row, length + row - turn)
        passed = (column >= 1) & (start + column - 1 <= limit)
        flags = jnp.where(column == 0, 1.0, jnp.where(passed, NEG, 0.0)).astype(jnp.bfloat16)

        def one_head(head):
            scores = scores_of(jnp.concatenate([queries_of(head), flags], axis=1), keys)
            before = peak[head]
            top = jnp.maximum(before, jnp.max(scores, axis=1, keepdims=True))
            spread_top = jnp.concatenate([top] * (width // HEAD_DIM), axis=1)
            weights = jnp.exp2((scores - spread_top) * scale).astype(jnp.bfloat16)
            factor = jnp.exp2((before - top) * scale)
            sums = total[head] * jnp.concatenate([factor] * 2, axis=1) + jnp.dot(
                weights, values, preferred_element_type=jnp.float32
            )
            if not last:
                peak[head] = top
                total[head] = sums
                return
            columns = slice(head * HEAD_DIM, (head + 1) * HEAD_DIM)
            result = sums[:, 0:HEAD_DIM] / sums[:, HEAD_DIM : 2 * HEAD_DIM]
            turn_out[:, columns] = jnp.where(shown, result[0:turn], 0.0).astype(jnp.bfloat16)
            decode_out[:, columns] = result[turn : turn + steps].astype(jnp.bfloat16)

        for head in range(heads):
            one_head(head)

    def round_trip(number, carry):
        @pl.when(number + AHEAD < whole)
        def _():
            spread(key_part(number + AHEAD))

        @pl.when(number < whole)
        def _():
            forward(key_part(number))

        for half in range(2):

            @pl.when(number + AHEAD == whole + half)
            def _():
                spread(end_part(half))

            @pl.when(number == whole + half)
            def _():
                forward(end_part(half))

        done = number - BEHIND
        consume(key_part(done), done * chunk, chunk, done, False)
        finish(key_part(done))
        return carry

    lax.fori_loop(BEHIND, whole + BEHIND, round_trip, 0)
    for half in range(2):
        consume(end_part(half), *cuts[whole + half], whole + half, half == 1)

    finish(end_part(0))
    finish(end_part(1))

    def finish_copies(number, carry):
        for copy in out_copies(number * chunk, chunk, number):
            copy.wait()
        return carry

    lax.fori_loop(0, whole, finish_copies, 0)
    for half in range(2):
        for copy in out_copies(*cuts[whole + half], whole + half):
            copy.wait()

    @pl.when(z == y)
    def _():
        for step in steps_out:
            for copy in small_copies(step):
                copy.wait_send()


def shards(
    cache_keys,
    cache_values,
    sink_keys,
    sink_values,
    turn_queries,
    turn_keys,
    turn_values,
    decode_queries,
    decode_keys,
    decode_values,
    turn_lengths,
    history,
    targets,
):
    ring = lax.axis_size("ctx")
    window_rows = cache_keys.shape[1]
    turn_rows = turn_keys.shape[1]
    columns = turn_queries.shape[2]
    heads = columns // HEAD_DIM
    steps = decode_queries.shape[1]
    query_rows = ring * turn_rows + PAD
    rows = (heads + 2) * turn_rows + 2 * window_rows
    small_rows = 4 * PAD + -(-heads * steps // PAD) * PAD
    count = heads // 2 + 2 + BLOCKS + 1
    arrays = (
        cache_keys,
        cache_values,
        sink_keys,
        sink_values,
        turn_queries,
        turn_keys,
        turn_values,
        decode_queries,
        decode_keys,
        decode_values,
    )
    vmem = pl.BlockSpec(memory_space=pltpu.VMEM)
    smem = pl.BlockSpec(memory_space=pltpu.SMEM)
    hbm = pl.BlockSpec(memory_space=pltpu.HBM)
    free = pl.BlockSpec(memory_space=pl.ANY)
    turn_out, decode_out, keys_out, values_out = pl.pallas_call(
        functools.partial(kernel, ring),
        out_shape=(
            jax.ShapeDtypeStruct((ring * turn_rows, columns), jnp.bfloat16),
            jax.ShapeDtypeStruct((steps, columns), jnp.bfloat16),
            jax.ShapeDtypeStruct((ring, window_rows, HEAD_DIM), jnp.bfloat16),
            jax.ShapeDtypeStruct((ring, window_rows, HEAD_DIM), jnp.bfloat16),
        ),
        in_specs=[smem] * 3 + [hbm] * 10,
        out_specs=(vmem, vmem, free, free),
        scratch_shapes=[
            pltpu.VMEM((ring, rows, HEAD_DIM), jnp.bfloat16),
            pltpu.VMEM((ring, rows, HEAD_DIM), jnp.bfloat16),
            pltpu.VMEM((ring, rows, HEAD_DIM), jnp.bfloat16),
            *[pltpu.VMEM(a.shape, a.dtype) for a in arrays],
            pltpu.SemaphoreType.DMA((len(arrays),)),
            pltpu.VMEM((ring, small_rows, HEAD_DIM), jnp.bfloat16),
            pltpu.VMEM((ring, 8, HEAD_DIM), jnp.int32),
            pltpu.VMEM((small_rows, HEAD_DIM), jnp.bfloat16),
            pltpu.VMEM((8, HEAD_DIM), jnp.int32),
            pltpu.VMEM((heads, PAD, HEAD_DIM), jnp.bfloat16),
            pltpu.VMEM((heads, query_rows, HEAD_DIM), jnp.float32),
            pltpu.VMEM((heads, query_rows, 2 * HEAD_DIM), jnp.float32),
            pltpu.VMEM((query_rows, ring * turn_rows + 2 * PAD), jnp.float32),
            pltpu.SemaphoreType.DMA((count, ring)),
            pltpu.SemaphoreType.DMA((count, ring)),
            pltpu.SemaphoreType.DMA((count, ring)),
            pltpu.SemaphoreType.DMA((count, ring)),
            pltpu.SemaphoreType.DMA((count,)),
            pltpu.SemaphoreType.DMA((2, ring)),
            pltpu.SemaphoreType.DMA((2,)),
            pltpu.SemaphoreType.DMA((2,)),
            pltpu.SemaphoreType.DMA((2, BLOCKS + 1)),
        ],
        compiler_params=pltpu.CompilerParams(
            collective_id=0, has_side_effects=True, vmem_limit_bytes=56 * 1024 * 1024
        ),
    )(
        turn_lengths,
        history,
        targets[:, 0],
        *arrays,
    )
    return (
        turn_out[None],
        decode_out[None],
        keys_out.reshape(1, ring * window_rows, HEAD_DIM),
        values_out.reshape(1, ring * window_rows, HEAD_DIM),
    )


def solution(mesh):
    whole = P("group", "ctx", "tensor")
    front = P("group", None, "tensor")
    slots = P(("group", "ctx"), None, "tensor")
    return jax.shard_map(
        shards,
        mesh=mesh,
        in_specs=(
            whole,
            whole,
            front,
            front,
            whole,
            whole,
            whole,
            front,
            front,
            front,
            P("group"),
            P("group"),
            P("group", None),
        ),
        out_specs=(slots,) * 4,
        check_vma=False,
    )
```

```python
import functools
import math

import jax
import jax.numpy as jnp
from jax import lax
from jax.experimental import pallas as pl
from jax.experimental.pallas import tpu as pltpu
from jax.sharding import PartitionSpec as P

HEAD_DIM = 128
SINKS = 4
NEG = -1e30
MESH = pl.DeviceIdType.MESH
PAD = 16
BLOCKS = 8
AHEAD = 3
BEHIND = 2


def kernel(
    ring,
    lengths,
    history,
    targets,
    cache_k_in,
    cache_v_in,
    sink_k_in,
    sink_v_in,
    turn_q_in,
    turn_k_in,
    turn_v_in,
    decode_q_in,
    decode_k_in,
    decode_v_in,
    turn_out,
    decode_out,
    keys_out,
    values_out,
    send,
    stage,
    final,
    cache_k,
    cache_v,
    sink_k,
    sink_v,
    turn_q,
    turn_k,
    turn_v,
    decode_q,
    decode_k,
    decode_v,
    in_sem,
    small_send,
    small_meta,
    small,
    meta,
    extra,
    peak,
    total,
    bias,
    z_send,
    z_recv,
    y_send,
    y_recv,
    own_sem,
    small_send_sem,
    small_recv_sem,
    small_own_sem,
    out_sem,
):
    z = lax.axis_index("group")
    tensor = lax.axis_index("tensor")
    y = lax.axis_index("ctx")
    sessions, window_rows, _ = cache_k.shape
    turn_rows = turn_k.shape[1]
    heads = turn_q.shape[2] // HEAD_DIM
    steps = decode_q.shape[1]
    window = window_rows * ring
    turn = turn_rows * ring
    query_rows = turn + PAD
    head_rows = (heads + 2) * turn_rows
    chunk = window_rows // BLOCKS
    whole = BLOCKS - 1
    query_stages = (heads + 2 - 2) // 2 + 2
    cuts = [(number * chunk, chunk) for number in range(whole)]
    cuts += [(whole * chunk + half * chunk // 2, chunk // 2) for half in range(2)]
    scale = math.log2(math.e) / math.sqrt(HEAD_DIM)

    def around(place, step):
        return lax.rem(place + step + ring, ring)

    def load(number, source, place):
        return pltpu.make_async_copy(source, place, in_sem.at[number])

    query_loads = (
        load(0, turn_q_in, turn_q),
        load(1, turn_k_in, turn_k),
        load(2, turn_v_in, turn_v),
    )
    window_loads = (load(3, cache_k_in, cache_k), load(4, cache_v_in, cache_v))
    small_loads = (
        load(5, sink_k_in, sink_k),
        load(6, sink_v_in, sink_v),
        load(7, decode_q_in, decode_q),
        load(8, decode_k_in, decode_k),
        load(9, decode_v_in, decode_v),
    )
    for copy in query_loads + small_loads + window_loads:
        copy.start()

    barrier = pltpu.get_barrier_semaphore()
    for step in range(1, ring):
        pl.semaphore_signal(
            barrier, inc=1, device_id=(around(z, step), tensor, y), device_id_type=MESH
        )
        pl.semaphore_signal(
            barrier, inc=1, device_id=(z, tensor, around(y, step)), device_id_type=MESH
        )

    def chosen(target):
        named = jnp.int32(0)
        active = jnp.int32(0)
        for s in range(sessions):
            hit = (targets[s] == target).astype(jnp.int32)
            named = jnp.maximum(named, s * hit)
            active = jnp.maximum(active, hit)
        return named, active

    def prepare_queries(step, place):
        named, active = chosen(around(z, step))
        live = active.astype(jnp.float32).astype(jnp.bfloat16)
        for head in range(heads):
            columns = slice(head * HEAD_DIM, (head + 1) * HEAD_DIM)
            rows = slice(head * turn_rows, (head + 1) * turn_rows)
            place[step, rows, :] = turn_q[named, :, columns] * live
        rows = slice(heads * turn_rows, (heads + 1) * turn_rows)
        place[step, rows, :] = turn_k[named] * live
        rows = slice((heads + 1) * turn_rows, (heads + 2) * turn_rows)
        place[step, rows, :] = turn_v[named] * live

    def prepare_window(step, place):
        named, active = chosen(around(z, step))
        live = active.astype(jnp.float32).astype(jnp.bfloat16)
        for start, size in cuts:
            rows = slice(start, start + size)
            first = head_rows + 2 * start
            place[step, first : first + size, :] = cache_k[named, rows, :] * live
            place[step, first + size : first + 2 * size, :] = cache_v[named, rows, :] * live

    def prepare(part):
        part(0, stage)

        def one_step(step, carry):
            part(step, send)
            return carry

        lax.fori_loop(1, ring, one_step, 0)

    def prepare_small(step, carry):
        named, active = chosen(around(z, step))
        live = active.astype(jnp.float32).astype(jnp.bfloat16)
        small_send[step] = jnp.zeros(small_send.shape[1:], jnp.bfloat16)
        small_send[step, 0:SINKS, :] = sink_k[named] * live
        small_send[step, PAD : PAD + steps, :] = decode_k[named] * live
        small_send[step, 2 * PAD : 2 * PAD + SINKS, :] = sink_v[named] * live
        small_send[step, 3 * PAD : 3 * PAD + steps, :] = decode_v[named] * live
        for head in range(heads):
            columns = slice(head * HEAD_DIM, (head + 1) * HEAD_DIM)
            start = 4 * PAD + head * steps
            small_send[step, start : start + steps, :] = decode_q[named, :, columns] * live
        first_row = lax.broadcasted_iota(jnp.int32, small_meta.shape[1:], 0) == 0
        small_meta[step] = jnp.where(first_row, history[named], lengths[named]) * active
        return carry

    for copy in query_loads:
        copy.wait()
    prepare(prepare_queries)

    pl.semaphore_wait(barrier, 2 * (ring - 1))

    def z_copy(number, place, size, step):
        rows = pl.ds(place, size)
        return pltpu.make_async_remote_copy(
            send.at[step, rows],
            stage.at[step, rows],
            z_send.at[number, step],
            z_recv.at[number, step],
            device_id=(around(z, step), tensor, y),
            device_id_type=MESH,
        )

    def y_copy(number, place, size, step, source, target):
        rows = pl.ds(place, size)
        return pltpu.make_async_remote_copy(
            stage.at[step, rows],
            final.at[source, rows],
            y_send.at[number, step],
            y_recv.at[number, source],
            device_id=(z, tensor, target),
            device_id_type=MESH,
        )

    def own_copy(number, place, size, step):
        rows = pl.ds(place, size)
        return pltpu.make_async_copy(
            stage.at[step, rows], final.at[y, rows], own_sem.at[number]
        )

    def short_part(number):
        return number, number * turn_rows, turn_rows

    def query_part(number):
        return number, pl.multiple_of((number - 1) * 2 * turn_rows, 16), 2 * turn_rows

    def key_part(number):
        place = pl.multiple_of(head_rows + number * 2 * chunk, 16)
        return number + query_stages, place, 2 * chunk

    def end_part(half):
        return query_stages + whole + half, head_rows + 2 * cuts[whole + half][0], chunk

    steps_out = sorted(range(1, ring), key=lambda step: -min(step, ring - step))
    steps_in = [0] + steps_out[::-1]

    def spread(part):
        for step in steps_out:
            z_copy(*part, step).start()

    def forward(part):
        for step in steps_in:
            home = around(z, -step)
            if step:
                z_copy(*part, step).wait_recv()

            @pl.when(home != y)
            def _():
                y_copy(*part, step, y, home).start()

            @pl.when(home == y)
            def _():
                own_copy(*part, step).start()

    def arrive(part):
        own_copy(*part, 0).wait()
        for step in range(1, ring):
            source = around(y, step)
            y_copy(*part, 0, source, source).wait_recv()

    def finish(part):
        for step in range(ring):
            if step:
                z_copy(*part, step).wait_send()
            home = around(z, -step)

            @pl.when(home != y)
            def _():
                y_copy(*part, step, y, home).wait_send()

    def small_copies(step):
        target = (around(z, step), tensor, y)
        return (
            pltpu.make_async_remote_copy(
                small_send.at[step],
                small,
                small_send_sem.at[0, step],
                small_recv_sem.at[0],
                device_id=target,
                device_id_type=MESH,
            ),
            pltpu.make_async_remote_copy(
                small_meta.at[step],
                meta,
                small_send_sem.at[1, step],
                small_recv_sem.at[1],
                device_id=target,
                device_id_type=MESH,
            ),
        )

    def small_own():
        return (
            pltpu.make_async_copy(small_send.at[0], small, small_own_sem.at[0]),
            pltpu.make_async_copy(small_meta.at[0], meta, small_own_sem.at[1]),
        )

    for part in (short_part(0), short_part(1), query_part(2)):
        spread(part)

    for copy in window_loads:
        copy.wait()
    prepare(prepare_window)
    for copy in small_loads:
        copy.wait()

    @pl.when(z == y)
    def _():
        lax.fori_loop(0, ring, prepare_small, 0)
        for step in steps_out:
            for copy in small_copies(step):
                copy.start()
        for copy in small_own():
            copy.start()

    def early(number, carry):
        spread(query_part(number + AHEAD))
        forward(query_part(number))
        return carry

    def late(number, carry):
        spread(key_part(number + AHEAD - query_stages))
        forward(query_part(number))
        return carry

    for number in range(2):
        spread(query_part(number + AHEAD))
        forward(short_part(number))
    lax.fori_loop(2, query_stages - AHEAD, early, 0)
    lax.fori_loop(query_stages - AHEAD, query_stages, late, 0)
    for number in range(BEHIND):
        spread(key_part(number + AHEAD))
        forward(key_part(number))

    def settle_queries(number, carry):
        arrive(query_part(number))
        finish(query_part(number))
        return carry

    for number in range(2):
        arrive(short_part(number))
        finish(short_part(number))
    lax.fori_loop(2, query_stages, settle_queries, 0)

    @pl.when(z == y)
    def _():
        for copy in small_own():
            copy.wait()

    @pl.when(z != y)
    def _():
        for copy in small_copies(1):
            copy.wait_recv()

    def block_of(place, size):
        return final[:, pl.ds(place, size), :].reshape(ring * size, HEAD_DIM)

    def queries_of(head):
        return jnp.concatenate([block_of(head * turn_rows, turn_rows), extra[head]], axis=0)

    def scores_of(queries, keys):
        return lax.dot_general(
            queries,
            keys,
            (((1,), (1,)), ((), ())),
            preferred_element_type=jnp.float32,
        )

    def with_ones(values):
        return jnp.concatenate([values, jnp.ones_like(values)], axis=1)

    prior = meta[0:1, 0:1]
    length = meta[1:2, 0:1]

    def row_numbers(shape):
        return lax.broadcasted_iota(jnp.int32, shape, 0)

    def column_numbers(shape):
        return lax.broadcasted_iota(jnp.int32, shape, 1)

    first = (query_rows, turn + 2 * PAD)
    row, column = row_numbers(first), column_numbers(first)
    in_turn = row < turn
    limit = jnp.where(in_turn, row, length - 1)
    number = column - turn - PAD
    sees = (
        ((column < turn) & (column <= limit))
        | ((column >= turn) & (column < turn + SINKS))
        | ((number >= 0) & (number < steps) & (number <= row - turn))
    )
    bias[...] = jnp.where(sees, 0.0, NEG)
    packed = small[4 * PAD :, :]
    shape = (PAD, packed.shape[0])
    row, column = row_numbers(shape), column_numbers(shape)
    for head in range(heads):
        picks = (row < steps) & (column == head * steps + row)
        picks = jnp.where(picks, 1.0, 0.0).astype(jnp.bfloat16)
        extra[head] = jnp.dot(picks, packed, preferred_element_type=jnp.float32).astype(
            jnp.bfloat16
        )
    first_keys = jnp.concatenate(
        [block_of(heads * turn_rows, turn_rows), small[0 : 2 * PAD, :]], axis=0
    )
    first_values = with_ones(
        jnp.concatenate(
            [block_of((heads + 1) * turn_rows, turn_rows), small[2 * PAD : 4 * PAD, :]], axis=0
        )
    )

    def start_head(head):
        scores = scores_of(queries_of(head), first_keys) + bias[...]
        top = jnp.max(scores, axis=1, keepdims=True)
        weights = jnp.exp2((scores - top) * scale).astype(jnp.bfloat16)
        peak[head] = jnp.broadcast_to(top, (query_rows, HEAD_DIM))
        total[head] = jnp.dot(weights, first_values, preferred_element_type=jnp.float32)

    for head in range(heads):
        start_head(head)

    shown = row_numbers((turn, HEAD_DIM)) < length

    def out_copies(start, size, number):
        place = head_rows + 2 * start
        rows = pl.ds(pl.multiple_of(start, 16), size)
        return (
            pltpu.make_async_copy(
                final.at[:, pl.ds(pl.multiple_of(place, 16), size)],
                keys_out.at[:, rows],
                out_sem.at[0, number],
            ),
            pltpu.make_async_copy(
                final.at[:, pl.ds(pl.multiple_of(place + size, 16), size)],
                values_out.at[:, rows],
                out_sem.at[1, number],
            ),
        )

    def consume(part, start, size, number, last):
        arrive(part)
        for copy in out_copies(start, size, number):
            copy.start()
        width = ring * size
        place = pl.multiple_of(head_rows + 2 * start, 16)
        values = with_ones(block_of(pl.multiple_of(place + size, 16), size))
        shape = (width, HEAD_DIM)
        row, column = row_numbers(shape), column_numbers(shape)
        position = lax.div(row, size) * window_rows + start + lax.rem(row, size)
        gone = (column == 0) & (position < window + SINKS - prior)
        marked = (column == row + 1) & (row < size)
        marks = jnp.where(gone, NEG, jnp.where(marked, 1.0, 0.0)).astype(jnp.bfloat16)
        keys = jnp.concatenate([block_of(place, size), marks], axis=1)
        shape = (query_rows, HEAD_DIM)
        row, column = row_numbers(shape), column_numbers(shape)
        limit = jnp.where(row < turn, row, length + row - turn)
        passed = (column >= 1) & (start + column - 1 <= limit)
        flags = jnp.where(column == 0, 1.0, jnp.where(passed, NEG, 0.0)).astype(jnp.bfloat16)

        def one_head(head):
            scores = scores_of(jnp.concatenate([queries_of(head), flags], axis=1), keys)
            before = peak[head]
            top = jnp.maximum(before, jnp.max(scores, axis=1, keepdims=True))
            spread_top = jnp.concatenate([top] * (width // HEAD_DIM), axis=1)
            weights = jnp.exp2((scores - spread_top) * scale).astype(jnp.bfloat16)
            factor = jnp.exp2((before - top) * scale)
            sums = total[head] * jnp.concatenate([factor] * 2, axis=1) + jnp.dot(
                weights, values, preferred_element_type=jnp.float32
            )
            if not last:
                peak[head] = top
                total[head] = sums
                return
            columns = slice(head * HEAD_DIM, (head + 1) * HEAD_DIM)
            result = sums[:, 0:HEAD_DIM] / sums[:, HEAD_DIM : 2 * HEAD_DIM]
            turn_out[:, columns] = jnp.where(shown, result[0:turn], 0.0).astype(jnp.bfloat16)
            decode_out[:, columns] = result[turn : turn + steps].astype(jnp.bfloat16)

        for head in range(heads):
            one_head(head)

    def round_trip(number, carry):
        @pl.when(number + AHEAD < whole)
        def _():
            spread(key_part(number + AHEAD))

        @pl.when(number < whole)
        def _():
            forward(key_part(number))

        for half in range(2):

            @pl.when(number + AHEAD == whole + half)
            def _():
                spread(end_part(half))

            @pl.when(number == whole + half)
            def _():
                forward(end_part(half))

        done = number - BEHIND
        consume(key_part(done), done * chunk, chunk, done, False)
        finish(key_part(done))
        return carry

    lax.fori_loop(BEHIND, whole + BEHIND, round_trip, 0)
    for half in range(2):
        consume(end_part(half), *cuts[whole + half], whole + half, half == 1)

    finish(end_part(0))
    finish(end_part(1))

    def finish_copies(number, carry):
        for copy in out_copies(number * chunk, chunk, number):
            copy.wait()
        return carry

    lax.fori_loop(0, whole, finish_copies, 0)
    for half in range(2):
        for copy in out_copies(*cuts[whole + half], whole + half):
            copy.wait()

    @pl.when(z == y)
    def _():
        for step in steps_out:
            for copy in small_copies(step):
                copy.wait_send()


PIECES = 4


def settle(
    turn_in,
    decode_in,
    keys_in,
    values_in,
    turn_out,
    decode_out,
    keys_out,
    values_out,
    turn_held,
    keys_held,
    values_held,
    come,
    gone,
):
    arriving, leaving = [], []
    for number, (source, held, place) in enumerate(
        (
            (keys_in, keys_held, keys_out),
            (values_in, values_held, values_out),
            (turn_in, turn_held, turn_out),
        )
    ):
        size = source.shape[0] // PIECES
        for piece in range(PIECES):
            rows = pl.ds(piece * size, size)
            arriving.append(
                pltpu.make_async_copy(source.at[rows], held.at[rows], come.at[number, piece])
            )
            leaving.append(
                pltpu.make_async_copy(held.at[rows], place.at[rows], gone.at[number, piece])
            )
    for copy in arriving:
        copy.start()
    decode_out[...] = decode_in[...]
    for before, after in zip(arriving, leaving):
        before.wait()
        after.start()
    for copy in leaving:
        copy.wait()


def shards(
    cache_keys,
    cache_values,
    sink_keys,
    sink_values,
    turn_queries,
    turn_keys,
    turn_values,
    decode_queries,
    decode_keys,
    decode_values,
    turn_lengths,
    history,
    targets,
):
    ring = lax.axis_size("ctx")
    window_rows = cache_keys.shape[1]
    turn_rows = turn_keys.shape[1]
    columns = turn_queries.shape[2]
    heads = columns // HEAD_DIM
    steps = decode_queries.shape[1]
    query_rows = ring * turn_rows + PAD
    rows = (heads + 2) * turn_rows + 2 * window_rows
    small_rows = 4 * PAD + -(-heads * steps // PAD) * PAD
    count = heads // 2 + 2 + BLOCKS + 1
    arrays = (
        cache_keys,
        cache_values,
        sink_keys,
        sink_values,
        turn_queries,
        turn_keys,
        turn_values,
        decode_queries,
        decode_keys,
        decode_values,
    )
    vmem = pl.BlockSpec(memory_space=pltpu.VMEM)
    smem = pl.BlockSpec(memory_space=pltpu.SMEM)
    hbm = pl.BlockSpec(memory_space=pltpu.HBM)
    free = pl.BlockSpec(memory_space=pl.ANY)
    outs = pl.pallas_call(
        functools.partial(kernel, ring),
        out_shape=(
            jax.ShapeDtypeStruct((ring * turn_rows, columns), jnp.bfloat16),
            jax.ShapeDtypeStruct((steps, columns), jnp.bfloat16),
            jax.ShapeDtypeStruct((ring, window_rows, HEAD_DIM), jnp.bfloat16),
            jax.ShapeDtypeStruct((ring, window_rows, HEAD_DIM), jnp.bfloat16),
        ),
        in_specs=[smem] * 3 + [hbm] * 10,
        out_specs=(vmem, vmem, free, free),
        scratch_shapes=[
            pltpu.VMEM((ring, rows, HEAD_DIM), jnp.bfloat16),
            pltpu.VMEM((ring, rows, HEAD_DIM), jnp.bfloat16),
            pltpu.VMEM((ring, rows, HEAD_DIM), jnp.bfloat16),
            *[pltpu.VMEM(a.shape, a.dtype) for a in arrays],
            pltpu.SemaphoreType.DMA((len(arrays),)),
            pltpu.VMEM((ring, small_rows, HEAD_DIM), jnp.bfloat16),
            pltpu.VMEM((ring, 8, HEAD_DIM), jnp.int32),
            pltpu.VMEM((small_rows, HEAD_DIM), jnp.bfloat16),
            pltpu.VMEM((8, HEAD_DIM), jnp.int32),
            pltpu.VMEM((heads, PAD, HEAD_DIM), jnp.bfloat16),
            pltpu.VMEM((heads, query_rows, HEAD_DIM), jnp.float32),
            pltpu.VMEM((heads, query_rows, 2 * HEAD_DIM), jnp.float32),
            pltpu.VMEM((query_rows, ring * turn_rows + 2 * PAD), jnp.float32),
            pltpu.SemaphoreType.DMA((count, ring)),
            pltpu.SemaphoreType.DMA((count, ring)),
            pltpu.SemaphoreType.DMA((count, ring)),
            pltpu.SemaphoreType.DMA((count, ring)),
            pltpu.SemaphoreType.DMA((count,)),
            pltpu.SemaphoreType.DMA((2, ring)),
            pltpu.SemaphoreType.DMA((2,)),
            pltpu.SemaphoreType.DMA((2,)),
            pltpu.SemaphoreType.DMA((2, BLOCKS + 1)),
        ],
        compiler_params=pltpu.CompilerParams(
            collective_id=0, has_side_effects=True, vmem_limit_bytes=56 * 1024 * 1024
        ),
    )(
        turn_lengths,
        history,
        targets[:, 0],
        *arrays,
    )
    turn_out, decode_out, keys_out, values_out = pl.pallas_call(
        settle,
        out_shape=tuple(jax.ShapeDtypeStruct(a.shape, a.dtype) for a in outs),
        in_specs=[hbm, vmem, hbm, hbm],
        out_specs=(hbm, vmem, hbm, hbm),
        scratch_shapes=[
            pltpu.VMEM(outs[0].shape, jnp.bfloat16),
            pltpu.VMEM(outs[2].shape, jnp.bfloat16),
            pltpu.VMEM(outs[3].shape, jnp.bfloat16),
            pltpu.SemaphoreType.DMA((3, PIECES)),
            pltpu.SemaphoreType.DMA((3, PIECES)),
        ],
        compiler_params=pltpu.CompilerParams(vmem_limit_bytes=56 * 1024 * 1024),
    )(*outs)
    return (
        turn_out[None],
        decode_out[None],
        keys_out.reshape(1, ring * window_rows, HEAD_DIM),
        values_out.reshape(1, ring * window_rows, HEAD_DIM),
    )


def solution(mesh):
    whole = P("group", "ctx", "tensor")
    front = P("group", None, "tensor")
    slots = P(("group", "ctx"), None, "tensor")
    return jax.shard_map(
        shards,
        mesh=mesh,
        in_specs=(
            whole,
            whole,
            front,
            front,
            whole,
            whole,
            whole,
            front,
            front,
            front,
            P("group"),
            P("group"),
            P("group", None),
        ),
        out_specs=(slots,) * 4,
        check_vma=False,
    )
```
